32 devices in a mesh: grp: 2 (over y), seq: 4 (over z), head: 2 (over x), sub: 2 (over core).
Axes of the slice: x: 2, y: 2, z: 4, core: 2. Of those that a mesh axis runs over, the one named last changes fastest.
Arguments:
- queries: bfloat16 [4096, 64, 128], P(('grp', 'seq'), ('head', 'sub')), parts along dimension 0, may hold values from -6 to 6
- key_rows: bfloat16 [4096, 64, 128], P(('grp', 'seq'), ('head', 'sub')), parts along dimension 0, may hold values from -6 to 6
- value_rows: bfloat16 [4096, 64, 128], P(('grp', 'seq'), ('head', 'sub')), parts along dimension 0, may hold values from -6 to 6
- out_adjoint: bfloat16 [4096, 64, 128], P(('grp', 'seq'), ('head', 'sub')), parts along dimension 0, may hold values from -6 to 6
Outputs:
- attended: bfloat16 [4096, 64, 128], P(('grp', 'seq'), ('head', 'sub')), parts along dimension 0
- query_grad: bfloat16 [4096, 64, 128], P(('grp', 'seq', 'head', 'sub')), parts along dimension 0
- key_grad: bfloat16 [4096, 64, 128], P(('grp', 'seq', 'head', 'sub')), parts along dimension 0
- value_grad: bfloat16 [4096, 64, 128], P(('grp', 'seq', 'head', 'sub')), parts along dimension 0
The draws below stay inside these ranges and needn't reach their ends.
There are 2 independent parts, one for each index of `grp`. The reference program is written for one: setup_inputs(seed, part) draws one part's arguments, and reference() takes and returns one part's arrays. A program takes and returns all parts, laid end to end along the dimension named above; each array names one. Nothing has to cross between parts.
All inputs are finite; a program needn't handle non-finite values.
Results may differ from the reference program's by a relative error of at most 0.0058.
Values may be sent and summed in bfloat16 or wider, within the bound.
A program may use at most 128 MiB of HBM per device.

```python
import jax
import jax.numpy as jnp
from jax import lax

HEADS = 64
HEAD_DIM = 128
SPAN = 64
TOKENS = 2048


def shard_levels(rng, dims, pieces, low, top_value):
    level = 1.0
    for dim, blocks in pieces:
        draws = jax.random.uniform(jax.random.fold_in(jax.random.fold_in(rng, 6), dim), (blocks,), jnp.float32, low / len(pieces), top_value / len(pieces))
        level = level * jnp.repeat(jnp.exp(draws), dims[dim] // blocks).reshape((-1,) + (1,) * (len(dims) - 1 - dim))
    return level


def bell_draw(rng, extent, width, reach, pieces=(), kind=jnp.bfloat16):
    level = shard_levels(rng, extent, pieces, -0.22, 0.18) if pieces else 1.0
    entries = jax.random.normal(rng, extent, jnp.float32) * width * level
    return jnp.minimum(jnp.maximum(entries, -reach), reach).astype(kind)


def setup_inputs(seed: int = 0, part: int = 0) -> dict:
    keys = jax.random.split(jax.random.key(seed), 5)
    part_splits = jax.random.split(jax.random.fold_in(keys[4], part), 5)
    return {
        "queries": bell_draw(part_splits[0], (TOKENS, HEADS, HEAD_DIM), 1.0, 6.0, ((0, 4), (1, 4))),
        "key_rows": bell_draw(part_splits[1], (TOKENS, HEADS, HEAD_DIM), 1.0, 6.0, ((0, 4), (1, 4))),
        "value_rows": bell_draw(part_splits[2], (TOKENS, HEADS, HEAD_DIM), 1.0, 6.0, ((0, 4), (1, 4))),
        "out_adjoint": bell_draw(part_splits[3], (TOKENS, HEADS, HEAD_DIM), 1.0, 6.0, ((0, 4), (1, 4))),
    }


def one_head(operands):
    queries, key_rows, value_rows, out_adjoint = operands
    blocks = TOKENS // SPAN
    position = jnp.arange(TOKENS, dtype=jnp.int32)
    factor = lax.rsqrt(jnp.float32(HEAD_DIM) * (position + 1).astype(jnp.float32))
    scaled = (queries.astype(jnp.float32) * factor[:, None]).astype(jnp.bfloat16)
    qsc = scaled.reshape(blocks, SPAN, HEAD_DIM).astype(jnp.float32)
    kch = key_rows.reshape(blocks, SPAN, HEAD_DIM).astype(jnp.float32)
    vch = value_rows.reshape(blocks, SPAN, HEAD_DIM).astype(jnp.float32)
    dch = out_adjoint.reshape(blocks, SPAN, HEAD_DIM).astype(jnp.float32)
    kv_block = jnp.einsum('ncd,nce->nde', kch, vch)
    state = jnp.cumsum(kv_block, 0) - kv_block
    state_low = state.astype(jnp.bfloat16).astype(jnp.float32)
    adj_block = jnp.einsum('nce,ncd->ned', dch, qsc)
    suffix = jnp.cumsum(adj_block[::-1], 0)[::-1] - adj_block
    suffix_low = suffix.astype(jnp.bfloat16).astype(jnp.float32)
    row = jnp.arange(SPAN, dtype=jnp.int32)
    causal = row[:, None] >= row[None, :]
    scores = jnp.where(causal[None], jnp.einsum('ncd,nsd->ncs', qsc, kch), 0.0)
    scores = scores.astype(jnp.bfloat16).astype(jnp.float32)
    attended = jnp.einsum('ncd,nde->nce', qsc, state_low) + jnp.einsum('ncs,nse->nce', scores, vch)
    adj_scores = jnp.where(causal[None], jnp.einsum('nce,nse->ncs', dch, vch), 0.0)
    adj_scores = adj_scores.astype(jnp.bfloat16).astype(jnp.float32)
    query_grad = (jnp.einsum('nce,nde->ncd', dch, state_low) + jnp.einsum('ncs,nsd->ncd', adj_scores, kch)) * factor.reshape(blocks, SPAN, 1)
    key_grad = jnp.einsum('nse,ned->nsd', vch, suffix_low) + jnp.einsum('ncs,ncd->nsd', adj_scores, qsc)
    value_grad = jnp.einsum('nsd,ned->nse', kch, suffix_low) + jnp.einsum('ncs,nce->nse', scores, dch)
    shape = (TOKENS, HEAD_DIM)
    return (attended.reshape(shape).astype(jnp.bfloat16), query_grad.reshape(shape).astype(jnp.bfloat16), key_grad.reshape(shape).astype(jnp.bfloat16), value_grad.reshape(shape).astype(jnp.bfloat16))

def reference(queries, key_rows, value_rows, out_adjoint):
    moved = (jnp.transpose(queries, (1, 0, 2)), jnp.transpose(key_rows, (1, 0, 2)), jnp.transpose(value_rows, (1, 0, 2)), jnp.transpose(out_adjoint, (1, 0, 2)))
    results = lax.map(one_head, moved)
    attended, query_grad, key_grad, value_grad = [jnp.transpose(r, (1, 0, 2)) for r in results]
    return (attended, query_grad, key_grad, value_grad)
```

```python
import functools

import jax
import jax.numpy as jnp
from jax import lax
from jax.experimental import pallas as pl
from jax.experimental.pallas import tpu as pltpu
from jax.sharding import PartitionSpec as P

MESH = pl.DeviceIdType.MESH
CHUNK = 128
GROUP = 2
F32 = jnp.float32
BF16 = jnp.bfloat16


def dot(a, b, da, db):
    return lax.dot_general(a, b, (((da,), (db,)), ((), ())), preferred_element_type=F32)


def main_kernel(
    nseq, nhead, nsub,
    k_hbm, v_hbm, d_hbm, q_hbm,
    att_out, qg_out, kg_out, vg_out,
    raw, kt, vt, dt, qt, fac, kv_loc, kv_tot, ad_loc, ad_tot,
    pre_in, pre_out, suf_in, suf_out, gq, gk, gv, att,
    in_sem, z_send, z_recv, x_send, x_recv, own_sem, att_sem,
):
    heads, tok, dim = kt.shape
    n = nhead * nsub
    tok_out = tok // n
    size = min(GROUP, heads)
    groups = heads // size
    chunks = tok // CHUNK
    seq = lax.axis_index("seq")
    sub = lax.axis_index("sub")
    me = lax.axis_index("head") * nsub + sub
    last = nseq - 1
    offsets = sorted(range(1, n), key=lambda o: -min(o, n - o))

    def mate(off):
        other = lax.rem(me + off, n)
        return other, {"head": other // nsub, "sub": lax.rem(other, nsub)}

    barrier = pltpu.get_barrier_semaphore()
    for off in offsets:
        pl.semaphore_signal(barrier, inc=1, device_id=mate(off)[1], device_id_type=MESH)

    @pl.when(seq > 0)
    def _():
        pl.semaphore_signal(barrier, inc=1, device_id={"seq": seq - 1}, device_id_type=MESH)

    @pl.when(seq < last)
    def _():
        pl.semaphore_signal(barrier, inc=1, device_id={"seq": seq + 1}, device_id_type=MESH)

    loads = [
        pltpu.make_async_copy(ref, raw.at[i], in_sem.at[i])
        for i, ref in enumerate((k_hbm, v_hbm, d_hbm, q_hbm))
    ]
    lower = seq < (nseq + 1) // 2

    @pl.when(lower)
    def _():
        for i in (0, 1, 2, 3):
            loads[i].start()

    @pl.when(jnp.logical_not(lower))
    def _():
        for i in (2, 3, 0, 1):
            loads[i].start()

    row = lax.broadcasted_iota(jnp.int32, (tok, dim), 0)
    fac[...] = lax.rsqrt(F32(dim) * (seq * tok + row + 1).astype(F32))

    @pl.when(seq == 0)
    def _():
        pre_in[...] = jnp.zeros_like(pre_in)

    @pl.when(seq == last)
    def _():
        suf_in[...] = jnp.zeros_like(suf_in)

    pl.semaphore_wait(
        barrier, n - 1 + (seq > 0).astype(jnp.int32) + (seq < last).astype(jnp.int32)
    )

    block = 64

    def turn(i, out, scale=False):
        loads[i].wait()

        def one(b, _):
            rows = pl.ds(pl.multiple_of(b * block, block), block)
            x = jnp.swapaxes(raw[i, rows], 0, 1)
            if scale:
                x = (x.astype(F32) * fac[rows][None]).astype(BF16)
            out[:, rows, :] = x
            return 0

        lax.fori_loop(0, tok // block, one, 0)

    def part(c):
        return pl.ds(c * CHUNK, CHUNK)

    def total_kv():
        def one(h, _):
            acc = jnp.zeros((dim, dim), F32)
            for c in range(chunks):
                kv_loc[h, c] = acc
                acc = acc + dot(kt[h, part(c)], vt[h, part(c)], 0, 0)
            kv_tot[h] = acc
            return 0

        lax.fori_loop(0, heads, one, 0)

    def total_ad():
        def one(h, _):
            acc = jnp.zeros((dim, dim), F32)
            for c in reversed(range(chunks)):
                ad_loc[h, c] = acc
                acc = acc + dot(dt[h, part(c)], qt[h, part(c)], 0, 0)
            ad_tot[h] = acc
            return 0

        lax.fori_loop(0, heads, one, 0)

    def group(g):
        return pl.ds(g * size, size)

    def chain(way, g):
        src, dst, to = (pre_out, pre_in, seq + 1) if way == 0 else (suf_out, suf_in, seq - 1)
        return pltpu.make_async_remote_copy(
            src_ref=src.at[group(g)],
            dst_ref=dst.at[group(g)],
            send_sem=z_send.at[way, g],
            recv_sem=z_recv.at[way, g],
            device_id={"seq": to},
            device_id_type=MESH,
        )

    def pass_on(way, g):
        src, dst, tot = (pre_out, pre_in, kv_tot) if way == 0 else (suf_out, suf_in, ad_tot)
        gets, gives = (seq > 0, seq < last) if way == 0 else (seq < last, seq > 0)

        @pl.when(gets)
        def _():
            chain(way, g).wait_recv()

        @pl.when(gives)
        def _():
            src[group(g)] = (dst[group(g)].astype(F32) + tot[group(g)]).astype(BF16)
            chain(way, g).start()

    grads = (gq, gk, gv)
    outs = (qg_out, kg_out, vg_out)

    def cross(a, g, off):
        other, ids = mate(off)
        return pltpu.make_async_remote_copy(
            src_ref=grads[a].at[group(g), pl.ds(pl.multiple_of(other * tok_out, tok_out), tok_out)],
            dst_ref=outs[a].at[me, group(g)],
            send_sem=x_send.at[a, g, other],
            recv_sem=x_recv.at[a, g, me],
            device_id=ids,
            device_id_type=MESH,
        )

    def cross_in(a, g, off):
        other, ids = mate(off)
        return pltpu.make_async_remote_copy(
            src_ref=grads[a].at[group(g), pl.ds(pl.multiple_of(other * tok_out, tok_out), tok_out)],
            dst_ref=outs[a].at[other, group(g)],
            send_sem=x_send.at[a, g, other],
            recv_sem=x_recv.at[a, g, other],
            device_id=ids,
            device_id_type=MESH,
        )

    def own(a, g):
        return pltpu.make_async_copy(
            grads[a].at[group(g), pl.ds(pl.multiple_of(me * tok_out, tok_out), tok_out)],
            outs[a].at[me, group(g)],
            own_sem.at[a, g],
        )

    def send(a, g):
        for off in offsets:
            cross(a, g, off).start()
        own(a, g).start()

    causal = lax.broadcasted_iota(jnp.int32, (CHUNK, CHUNK), 0) >= lax.broadcasted_iota(
        jnp.int32, (CHUNK, CHUNK), 1
    )

    def masked(a, b):
        return jnp.where(causal, dot(a, b, 1, 1), 0.0).astype(BF16)

    def loop_q():
        def one(g, _):
            pass_on(0, g)
            for i in range(size):
                h = g * size + i
                before = pre_in[h].astype(F32)
                for c in range(chunks):
                    state = (before + kv_loc[h, c]).astype(BF16)
                    d = dt[h, part(c)]
                    adj = masked(d, vt[h, part(c)])
                    out = dot(d, state, 1, 1) + dot(adj, kt[h, part(c)], 1, 0)
                    gq[h, part(c)] = (out * fac[part(c)]).astype(BF16)
            send(0, g)
            return 0

        lax.fori_loop(0, groups, one, 0)

    def loop_kv():
        def one(g, _):
            pass_on(1, g)
            for i in range(size):
                h = g * size + i
                after = suf_in[h].astype(F32)
                for c in range(chunks):
                    state = (after + ad_loc[h, c]).astype(BF16)
                    q, k, v, d = (x[h, part(c)] for x in (qt, kt, vt, dt))
                    adj = masked(d, v)
                    scores = masked(q, k)
                    gk[h, part(c)] = (dot(v, state, 1, 0) + dot(adj, q, 0, 0)).astype(BF16)
                    gv[h, part(c)] = (dot(k, state, 1, 1) + dot(scores, d, 0, 0)).astype(BF16)
            send(1, g)
            send(2, g)
            return 0

        lax.fori_loop(0, groups, one, 0)

    @pl.when(lower)
    def _():
        turn(0, kt)
        turn(1, vt)
        total_kv()
        turn(2, dt)
        loop_q()
        turn(3, qt, True)
        total_ad()
        loop_kv()

    @pl.when(jnp.logical_not(lower))
    def _():
        turn(2, dt)
        turn(3, qt, True)
        total_ad()
        turn(0, kt)
        turn(1, vt)
        loop_kv()
        total_kv()
        loop_q()

    def write(g):
        return pltpu.make_async_copy(att.at[group(g)], att_out.at[group(g)], att_sem.at[g])

    def attend(g, _):
        for i in range(size):
            h = g * size + i
            before = pre_in[h].astype(F32)
            for c in range(chunks):
                state = (before + kv_loc[h, c]).astype(BF16)
                q = qt[h, part(c)]
                scores = masked(q, kt[h, part(c)])
                out = dot(q, state, 1, 0) + dot(scores, vt[h, part(c)], 1, 0)
                att[h, part(c)] = out.astype(BF16)
        write(g).start()
        return 0

    lax.fori_loop(0, groups, attend, 0)

    def drain(g, _):
        @pl.when(seq < last)
        def _():
            chain(0, g).wait_send()

        @pl.when(seq > 0)
        def _():
            chain(1, g).wait_send()

        write(g).wait()
        for a in range(3):
            own(a, g).wait()
            for off in offsets:
                copy = cross_in(a, g, off)
                copy.wait_send()
                copy.wait_recv()
        return 0

    lax.fori_loop(0, groups, drain, 0)


def exchange(nseq, nhead, nsub, queries, key_rows, value_rows, out_adjoint):
    tok, heads, dim = queries.shape
    n = nhead * nsub
    chunks = tok // CHUNK
    groups = heads // min(GROUP, heads)
    turned = pltpu.VMEM((heads, tok, dim), BF16)
    low = pltpu.VMEM((heads, dim, dim), BF16)
    any_spec = pl.BlockSpec(memory_space=pl.ANY)
    grad = jax.ShapeDtypeStruct((n, heads, tok // n, dim), BF16)
    return pl.pallas_call(
        functools.partial(main_kernel, nseq, nhead, nsub),
        out_shape=(jax.ShapeDtypeStruct((heads, tok, dim), BF16), grad, grad, grad),
        in_specs=[any_spec] * 4,
        out_specs=(any_spec,) * 4,
        scratch_shapes=[
            pltpu.VMEM((4, tok, heads, dim), BF16),
            turned, turned, turned, turned,
            pltpu.VMEM((tok, dim), F32),
            pltpu.VMEM((heads, chunks, dim, dim), F32),
            pltpu.VMEM((heads, dim, dim), F32),
            pltpu.VMEM((heads, chunks, dim, dim), F32),
            pltpu.VMEM((heads, dim, dim), F32),
            low, low, low, low,
            turned, turned, turned, turned,
            pltpu.SemaphoreType.DMA((4,)),
            pltpu.SemaphoreType.DMA((2, groups)),
            pltpu.SemaphoreType.DMA((2, groups)),
            pltpu.SemaphoreType.DMA((3, groups, n)),
            pltpu.SemaphoreType.DMA((3, groups, n)),
            pltpu.SemaphoreType.DMA((3, groups)),
            pltpu.SemaphoreType.DMA((groups,)),
        ],
        compiler_params=pltpu.CompilerParams(
            collective_id=0, has_side_effects=True, vmem_limit_bytes=50 * 2**20
        ),
    )(key_rows, value_rows, out_adjoint, queries)


def finish_kernel(att, a, b, c, att_out, a_out, b_out, c_out):
    att_out[...] = jnp.swapaxes(att[...], 0, 1)
    for src, dst in ((a, a_out), (b, b_out), (c, c_out)):
        n, heads, rows, dim = src.shape
        dst[...] = jnp.swapaxes(src[...].reshape(n * heads, rows, dim), 0, 1)


def finish(att, *grads):
    heads, tok, dim = att.shape
    n, _, rows, _ = grads[0].shape
    steps = max(1, rows // 16)
    tb, rb = tok // steps, rows // steps
    return pl.pallas_call(
        finish_kernel,
        grid=(steps,),
        out_shape=(jax.ShapeDtypeStruct((tok, heads, dim), BF16),)
        + (jax.ShapeDtypeStruct((rows, n * heads, dim), BF16),) * 3,
        in_specs=[pl.BlockSpec((heads, tb, dim), lambda i: (0, i, 0))]
        + [pl.BlockSpec((n, heads, rb, dim), lambda i: (0, 0, i, 0))] * 3,
        out_specs=(pl.BlockSpec((tb, heads, dim), lambda i: (i, 0, 0)),)
        + (pl.BlockSpec((rb, n * heads, dim), lambda i: (i, 0, 0)),) * 3,
        compiler_params=pltpu.CompilerParams(vmem_limit_bytes=32 * 2**20),
    )(att, *grads)


def solution(mesh):
    spec = P(("grp", "seq"), ("head", "sub"), None)
    grad = P(("grp", "seq", "head", "sub"), None, None)

    def per_device(queries, key_rows, value_rows, out_adjoint):
        return finish(
            *exchange(
                mesh.shape["seq"], mesh.shape["head"], mesh.shape["sub"],
                queries, key_rows, value_rows, out_adjoint,
            )
        )

    return jax.shard_map(
        per_device, mesh=mesh, in_specs=(spec,) * 4, out_specs=(spec, grad, grad, grad),
        check_vma=False,
    )
```

```python
import functools

import jax
import jax.numpy as jnp
from jax import lax
from jax.experimental import pallas as pl
from jax.experimental.pallas import tpu as pltpu
from jax.sharding import PartitionSpec as P

MESH = pl.DeviceIdType.MESH
CHUNK = 128
GROUP = 2
F32 = jnp.float32
BF16 = jnp.bfloat16


def dot(a, b, da, db):
    return lax.dot_general(a, b, (((da,), (db,)), ((), ())), preferred_element_type=F32)


def main_kernel(
    nseq, nhead, nsub,
    k_hbm, v_hbm, d_hbm, q_hbm,
    att_out, grad_out,
    raw, kt, vt, dt, qt, fac, kv_loc, kv_tot, ad_loc, ad_tot,
    pre_in, pre_out, suf_in, suf_out, grads, held, stage, att,
    in_sem, z_send, z_recv, x_send, x_recv, own_sem, att_sem, out_sem,
):
    heads, tok, dim = kt.shape
    n = nhead * nsub
    tok_out = tok // n
    size = min(GROUP, heads)
    groups = heads // size
    chunks = tok // CHUNK
    seq = lax.axis_index("seq")
    me = lax.axis_index("head") * nsub + lax.axis_index("sub")
    last = nseq - 1
    offsets = sorted(range(1, n), key=lambda o: -min(o, n - o))

    def mate(off):
        other = lax.rem(me + off, n)
        return other, {"head": other // nsub, "sub": lax.rem(other, nsub)}

    barrier = pltpu.get_barrier_semaphore()
    for off in offsets:
        pl.semaphore_signal(barrier, inc=1, device_id=mate(off)[1], device_id_type=MESH)

    @pl.when(seq > 0)
    def _():
        pl.semaphore_signal(barrier, inc=1, device_id={"seq": seq - 1}, device_id_type=MESH)

    @pl.when(seq < last)
    def _():
        pl.semaphore_signal(barrier, inc=1, device_id={"seq": seq + 1}, device_id_type=MESH)

    lower = seq < (nseq + 1) // 2
    upper = jnp.logical_not(lower)
    sources = (k_hbm, v_hbm, d_hbm, q_hbm)

    def load(i, c):
        rows = pl.ds(pl.multiple_of(c * CHUNK, CHUNK), CHUNK)
        return pltpu.make_async_copy(sources[i].at[rows], raw.at[i, rows], in_sem.at[i, c])

    def load_all(order):
        for i in order:
            for c in range(chunks):
                load(i, c).start()

    @pl.when(lower)
    def _():
        load_all((0, 1, 2, 3))

    @pl.when(upper)
    def _():
        load_all((2, 3, 1, 0))

    row = lax.broadcasted_iota(jnp.int32, (tok, dim), 0)
    fac[...] = lax.rsqrt(F32(dim) * (seq * tok + row + 1).astype(F32))

    @pl.when(seq == 0)
    def _():
        pre_in[...] = jnp.zeros_like(pre_in)

    @pl.when(seq == last)
    def _():
        suf_in[...] = jnp.zeros_like(suf_in)

    block = 64

    def turn(i, out, scale=False):
        def one(c, _):
            load(i, c).wait()
            for b in range(CHUNK // block):
                rows = pl.ds(pl.multiple_of(c * CHUNK + b * block, block), block)
                x = jnp.swapaxes(raw[i, rows], 0, 1)
                if scale:
                    x = (x.astype(F32) * fac[rows][None]).astype(BF16)
                out[:, rows, :] = x
            return 0

        lax.fori_loop(0, chunks, one, 0)

    def part(c):
        return pl.ds(c * CHUNK, CHUNK)

    def group(g):
        return pl.ds(g * size, size)

    def chain(way, g):
        src, dst, to = (pre_out, pre_in, seq + 1) if way == 0 else (suf_out, suf_in, seq - 1)
        return pltpu.make_async_remote_copy(
            src_ref=src.at[group(g)],
            dst_ref=dst.at[group(g)],
            send_sem=z_send.at[way, g],
            recv_sem=z_recv.at[way, g],
            device_id={"seq": to},
            device_id_type=MESH,
        )

    def ends(way):
        return (seq > 0, seq < last) if way == 0 else (seq < last, seq > 0)

    def total(way, g):
        left, right, loc, tot, out = (
            (kt, vt, kv_loc, kv_tot, pre_out) if way == 0 else (dt, qt, ad_loc, ad_tot, suf_out)
        )
        for i in range(size):
            h = g * size + i
            acc = jnp.zeros((dim, dim), F32)
            for c in range(chunks) if way == 0 else reversed(range(chunks)):
                loc[h, c] = acc
                acc = acc + dot(left[h, part(c)], right[h, part(c)], 0, 0)
            tot[h] = acc
        gets, gives = ends(way)

        @pl.when(jnp.logical_and(jnp.logical_not(gets), gives))
        def _():
            out[group(g)] = tot[group(g)].astype(BF16)
            chain(way, g).start()

    def pass_on(way, g):
        src, dst, tot = (pre_out, pre_in, kv_tot) if way == 0 else (suf_out, suf_in, ad_tot)
        gets, gives = ends(way)

        @pl.when(gets)
        def _():
            chain(way, g).wait_recv()

        @pl.when(jnp.logical_and(gets, gives))
        def _():
            src[group(g)] = (dst[group(g)].astype(F32) + tot[group(g)]).astype(BF16)
            chain(way, g).start()

    def mine(a, g, other):
        rows = pl.ds(pl.multiple_of(other * tok_out, tok_out), tok_out)
        return grads.at[a, group(g), rows]

    def cross(a, g, off, arriving=False):
        other, ids = mate(off)
        src = other if arriving else me
        return pltpu.make_async_remote_copy(
            src_ref=mine(a, g, other),
            dst_ref=held.at[a, src, group(g)],
            send_sem=x_send.at[a, g, other],
            recv_sem=x_recv.at[a, g, src],
            device_id=ids,
            device_id_type=MESH,
        )

    def own(a, g):
        return pltpu.make_async_copy(mine(a, g, me), held.at[a, me, group(g)], own_sem.at[a, g])

    def send(a, g):
        for off in offsets:
            cross(a, g, off).start()
        own(a, g).start()

    across = lax.broadcasted_iota(jnp.int32, (CHUNK, CHUNK), 0)
    along = lax.broadcasted_iota(jnp.int32, (CHUNK, CHUNK), 1)

    def masked(a, b):
        return jnp.where(across >= along, dot(a, b, 1, 1), 0.0).astype(BF16)

    def masked_t(a, b):
        return jnp.where(across <= along, dot(a, b, 1, 1), 0.0).astype(BF16)

    def walk(way, a, first, compute):
        if first:
            total(way, 0)

        def one(g, _):
            if first:
                @pl.when(g + 1 < groups)
                def _():
                    total(way, g + 1)

                pass_on(way, g)
            edge, loc = (pre_in, kv_loc) if way == 0 else (suf_in, ad_loc)
            for i in range(size):
                h = g * size + i
                outer = edge[h].astype(F32)
                for c in range(chunks):
                    state = (outer + loc[h, c]).astype(BF16)
                    grads[a, h, part(c)] = compute(h, c, state).astype(BF16)
            send(a, g)
            return 0

        lax.fori_loop(0, groups, one, 0)

    def query_part(h, c, state):
        d = dt[h, part(c)]
        adj = masked(d, vt[h, part(c)])
        return (dot(d, state, 1, 1) + dot(adj, kt[h, part(c)], 1, 0)) * fac[part(c)]

    def key_part(h, c, state):
        v = vt[h, part(c)]
        adj = masked_t(v, dt[h, part(c)])
        return dot(v, state, 1, 0) + dot(adj, qt[h, part(c)], 1, 0)

    def value_part(h, c, state):
        k = kt[h, part(c)]
        scores = masked_t(k, qt[h, part(c)])
        return dot(k, state, 1, 1) + dot(scores, dt[h, part(c)], 1, 0)

    @pl.when(lower)
    def _():
        turn(0, kt)
        turn(1, vt)
        turn(2, dt)

    @pl.when(upper)
    def _():
        turn(2, dt)
        turn(3, qt, True)
        turn(1, vt)

    pl.semaphore_wait(
        barrier, n - 1 + (seq > 0).astype(jnp.int32) + (seq < last).astype(jnp.int32)
    )

    @pl.when(lower)
    def _():
        walk(0, 0, True, query_part)
        turn(3, qt, True)
        walk(1, 1, True, key_part)
        walk(1, 2, False, value_part)

    @pl.when(upper)
    def _():
        walk(1, 1, True, key_part)
        turn(0, kt)
        walk(1, 2, False, value_part)
        walk(0, 0, True, query_part)

    def attend(g, _):
        for i in range(size):
            h = g * size + i
            before = pre_in[h].astype(F32)
            for c in range(chunks):
                state = (before + kv_loc[h, c]).astype(BF16)
                q = qt[h, part(c)]
                scores = masked(q, kt[h, part(c)])
                out = dot(q, state, 1, 0) + dot(scores, vt[h, part(c)], 1, 0)
                att[h, part(c)] = out.astype(BF16)
        return 0

    lax.fori_loop(0, groups, attend, 0)

    def turn_att(c, _):
        rows = pl.ds(pl.multiple_of(c * block, block), block)
        raw[0, rows] = jnp.swapaxes(att[:, rows, :], 0, 1)
        return 0

    lax.fori_loop(0, tok // block, turn_att, 0)
    att_copy = pltpu.make_async_copy(raw.at[0], att_out, att_sem)
    att_copy.start()

    strip = min(16, tok_out)
    strips = tok_out // strip

    def put(a, slot, r):
        rows = pl.ds(pl.multiple_of(r * strip, strip), strip)
        return pltpu.make_async_copy(
            stage.at[slot, rows], grad_out.at[a, rows], out_sem.at[slot, r]
        )

    def gather(i, _):
        a = lax.rem(i + upper.astype(jnp.int32), 3)
        slot = lax.rem(i, 2)

        def arrive(g, _):
            own(a, g).wait()
            for off in offsets:
                cross(a, g, off, True).wait_recv()
            return 0

        lax.fori_loop(0, groups, arrive, 0)

        @pl.when(i >= 2)
        def _():
            for r in range(strips):
                put(a, slot, r).wait()

        def one(r, _):
            rows = pl.ds(pl.multiple_of(r * strip, strip), strip)
            x = held[a, :, :, rows, :].reshape(n * heads, strip, dim)
            stage[slot, rows] = jnp.swapaxes(x, 0, 1)
            put(a, slot, r).start()
            return 0

        lax.fori_loop(0, strips, one, 0)
        return 0

    lax.fori_loop(0, 3, gather, 0)

    def drain(g, _):
        @pl.when(seq < last)
        def _():
            chain(0, g).wait_send()

        @pl.when(seq > 0)
        def _():
            chain(1, g).wait_send()

        for a in range(3):
            for off in offsets:
                cross(a, g, off).wait_send()
        return 0

    lax.fori_loop(0, groups, drain, 0)
    for slot in range(2):
        for r in range(strips):
            put(0, slot, r).wait()
    att_copy.wait()


def exchange(nseq, nhead, nsub, queries, key_rows, value_rows, out_adjoint):
    tok, heads, dim = queries.shape
    n = nhead * nsub
    tok_out = tok // n
    chunks = tok // CHUNK
    groups = heads // min(GROUP, heads)
    turned = pltpu.VMEM((heads, tok, dim), BF16)
    low = pltpu.VMEM((heads, dim, dim), BF16)
    any_spec = pl.BlockSpec(memory_space=pl.ANY)
    return pl.pallas_call(
        functools.partial(main_kernel, nseq, nhead, nsub),
        out_shape=(
            pltpu.VMEM((tok, heads, dim), BF16),
            pltpu.VMEM((3, tok_out, n * heads, dim), BF16),
        ),
        in_specs=[any_spec] * 4,
        out_specs=(any_spec,) * 2,
        scratch_shapes=[
            pltpu.VMEM((4, tok, heads, dim), BF16),
            turned, turned, turned, turned,
            pltpu.VMEM((tok, dim), F32),
            pltpu.VMEM((heads, chunks, dim, dim), F32),
            pltpu.VMEM((heads, dim, dim), F32),
            pltpu.VMEM((heads, chunks, dim, dim), F32),
            pltpu.VMEM((heads, dim, dim), F32),
            low, low, low, low,
            pltpu.VMEM((3, heads, tok, dim), BF16),
            pltpu.VMEM((3, n, heads, tok_out, dim), BF16),
            pltpu.VMEM((2, tok_out, n * heads, dim), BF16),
            turned,
            pltpu.SemaphoreType.DMA((4, chunks)),
            pltpu.SemaphoreType.DMA((2, groups)),
            pltpu.SemaphoreType.DMA((2, groups)),
            pltpu.SemaphoreType.DMA((3, groups, n)),
            pltpu.SemaphoreType.DMA((3, groups, n)),
            pltpu.SemaphoreType.DMA((3, groups)),
            pltpu.SemaphoreType.DMA,
            pltpu.SemaphoreType.DMA((2, tok_out // min(16, tok_out))),
        ],
        compiler_params=pltpu.CompilerParams(
            collective_id=0, has_side_effects=True, vmem_limit_bytes=50 * 2**20
        ),
    )(key_rows, value_rows, out_adjoint, queries)


def finish_kernel(pieces, att, grads, att_out, a_out, b_out, c_out, sem):
    outs = (att_out, a_out, b_out, c_out)
    copies = []
    for i, dst in enumerate(outs):
        src = att if i == 0 else grads.at[i - 1]
        step = dst.shape[0] // pieces
        for p in range(pieces):
            rows = pl.ds(p * step, step)
            copies.append(pltpu.make_async_copy(src.at[rows], dst.at[rows], sem.at[i, p]))
    for copy in copies:
        copy.start()
    for copy in copies:
        copy.wait()


def finish(att, grads):
    pieces = 4
    any_spec = pl.BlockSpec(memory_space=pl.ANY)
    return pl.pallas_call(
        functools.partial(finish_kernel, pieces),
        out_shape=(jax.ShapeDtypeStruct(att.shape, BF16),)
        + (jax.ShapeDtypeStruct(grads.shape[1:], BF16),) * 3,
        in_specs=[any_spec] * 2,
        out_specs=(any_spec,) * 4,
        scratch_shapes=[pltpu.SemaphoreType.DMA((4, pieces))],
        compiler_params=pltpu.CompilerParams(vmem_limit_bytes=2**20),
    )(att, grads)


def solution(mesh):
    spec = P(("grp", "seq"), ("head", "sub"), None)
    grad = P(("grp", "seq", "head", "sub"), None, None)

    def per_device(queries, key_rows, value_rows, out_adjoint):
        return finish(
            *exchange(
                mesh.shape["seq"], mesh.shape["head"], mesh.shape["sub"],
                queries, key_rows, value_rows, out_adjoint,
            )
        )

    return jax.shard_map(
        per_device, mesh=mesh, in_specs=(spec,) * 4, out_specs=(spec, grad, grad, grad),
        check_vma=False,
    )
```

```python
import functools

import jax
import jax.numpy as jnp
from jax import lax
from jax.experimental import pallas as pl
from jax.experimental.pallas import tpu as pltpu
from jax.sharding import PartitionSpec as P

MESH = pl.DeviceIdType.MESH
CHUNK = 128
GROUP = 2
F32 = jnp.float32
BF16 = jnp.bfloat16


def dot(a, b, da, db):
    return lax.dot_general(a, b, (((da,), (db,)), ((), ())), preferred_element_type=F32)


def main_kernel(
    nseq, nhead, nsub,
    k_hbm, v_hbm, d_hbm, q_hbm,
    att_out, grad_out,
    raw, kt, vt, dt, qt, fac, kv_loc, kv_tot, ad_loc, ad_tot,
    pre_in, pre_out, suf_in, suf_out, grads, held, stage, att,
    in_sem, z_send, z_recv, x_send, x_recv, own_sem, att_sem, out_sem,
):
    heads, tok, dim = kt.shape
    n = nhead * nsub
    tok_out = tok // n
    size = min(GROUP, heads)
    groups = heads // size
    chunks = tok // CHUNK
    seq = lax.axis_index("seq")
    me = lax.axis_index("head") * nsub + lax.axis_index("sub")
    last = nseq - 1
    offsets = sorted(range(1, n), key=lambda o: -min(o, n - o))

    def mate(off):
        other = lax.rem(me + off, n)
        return other, {"head": other // nsub, "sub": lax.rem(other, nsub)}

    barrier = pltpu.get_barrier_semaphore()
    for off in offsets:
        pl.semaphore_signal(barrier, inc=1, device_id=mate(off)[1], device_id_type=MESH)

    @pl.when(seq > 0)
    def _():
        pl.semaphore_signal(barrier, inc=1, device_id={"seq": seq - 1}, device_id_type=MESH)

    @pl.when(seq < last)
    def _():
        pl.semaphore_signal(barrier, inc=1, device_id={"seq": seq + 1}, device_id_type=MESH)

    lower = seq < (nseq + 1) // 2
    upper = jnp.logical_not(lower)
    sources = (k_hbm, v_hbm, d_hbm, q_hbm)

    def load(i, c):
        rows = pl.ds(pl.multiple_of(c * CHUNK, CHUNK), CHUNK)
        return pltpu.make_async_copy(sources[i].at[rows], raw.at[i, rows], in_sem.at[i, c])

    def load_all(order):
        for i in order:
            for c in range(chunks):
                load(i, c).start()

    @pl.when(lower)
    def _():
        load_all((0, 1, 2, 3))

    @pl.when(upper)
    def _():
        load_all((2, 3, 1, 0))

    row = lax.broadcasted_iota(jnp.int32, (tok, dim), 0)
    fac[...] = lax.rsqrt(F32(dim) * (seq * tok + row + 1).astype(F32))

    @pl.when(seq == 0)
    def _():
        pre_in[...] = jnp.zeros_like(pre_in)

    @pl.when(seq == last)
    def _():
        suf_in[...] = jnp.zeros_like(suf_in)

    block = 64

    halves = 2 if heads % 16 == 0 else 1
    half = heads // halves
    half_groups = groups // halves

    def some(p):
        return pl.ds(p * half, half)

    def turn(i, p, wait=False):
        out = (kt, vt, dt, qt)[i]

        def one(c, _):
            if wait:
                load(i, c).wait()
            for b in range(CHUNK // block):
                rows = pl.ds(pl.multiple_of(c * CHUNK + b * block, block), block)
                x = jnp.swapaxes(raw[i, rows, some(p), :], 0, 1)
                if i == 3:
                    x = (x.astype(F32) * fac[rows][None]).astype(BF16)
                out[some(p), rows, :] = x
            return 0

        lax.fori_loop(0, chunks, one, 0)

    def part(c):
        return pl.ds(c * CHUNK, CHUNK)

    def group(g):
        return pl.ds(g * size, size)

    def chain(way, g):
        src, dst, to = (pre_out, pre_in, seq + 1) if way == 0 else (suf_out, suf_in, seq - 1)
        return pltpu.make_async_remote_copy(
            src_ref=src.at[group(g)],
            dst_ref=dst.at[group(g)],
            send_sem=z_send.at[way, g],
            recv_sem=z_recv.at[way, g],
            device_id={"seq": to},
            device_id_type=MESH,
        )

    def ends(way):
        return (seq > 0, seq < last) if way == 0 else (seq < last, seq > 0)

    def total(way, g):
        left, right, loc, tot, out = (
            (kt, vt, kv_loc, kv_tot, pre_out) if way == 0 else (dt, qt, ad_loc, ad_tot, suf_out)
        )
        for i in range(size):
            h = g * size + i
            acc = jnp.zeros((dim, dim), F32)
            for c in range(chunks) if way == 0 else reversed(range(chunks)):
                loc[h, c] = acc
                acc = acc + dot(left[h, part(c)], right[h, part(c)], 0, 0)
            tot[h] = acc
        gets, gives = ends(way)

        @pl.when(jnp.logical_and(jnp.logical_not(gets), gives))
        def _():
            out[group(g)] = tot[group(g)].astype(BF16)
            chain(way, g).start()

    def pass_on(way, g):
        src, dst, tot = (pre_out, pre_in, kv_tot) if way == 0 else (suf_out, suf_in, ad_tot)
        gets, gives = ends(way)

        @pl.when(gets)
        def _():
            chain(way, g).wait_recv()

        @pl.when(jnp.logical_and(gets, gives))
        def _():
            src[group(g)] = (dst[group(g)].astype(F32) + tot[group(g)]).astype(BF16)
            chain(way, g).start()

    def mine(a, g, other):
        rows = pl.ds(pl.multiple_of(other * tok_out, tok_out), tok_out)
        return grads.at[a, group(g), rows]

    def cross(a, g, off, arriving=False):
        other, ids = mate(off)
        src = other if arriving else me
        return pltpu.make_async_remote_copy(
            src_ref=mine(a, g, other),
            dst_ref=held.at[a, src, group(g)],
            send_sem=x_send.at[a, g, other],
            recv_sem=x_recv.at[a, g, src],
            device_id=ids,
            device_id_type=MESH,
        )

    def own(a, g):
        return pltpu.make_async_copy(mine(a, g, me), held.at[a, me, group(g)], own_sem.at[a, g])

    def send(a, g):
        for off in offsets:
            cross(a, g, off).start()
        own(a, g).start()

    across = lax.broadcasted_iota(jnp.int32, (CHUNK, CHUNK), 0)
    along = lax.broadcasted_iota(jnp.int32, (CHUNK, CHUNK), 1)

    def masked(a, b):
        return jnp.where(across >= along, dot(a, b, 1, 1), 0.0).astype(BF16)

    def masked_t(a, b):
        return jnp.where(across <= along, dot(a, b, 1, 1), 0.0).astype(BF16)

    def walk(way, a, compute, begin, end, first):
        def one(g, _):
            if first:
                @pl.when(g + 1 < end)
                def _():
                    total(way, g + 1)

                pass_on(way, g)
            edge, loc = (pre_in, kv_loc) if way == 0 else (suf_in, ad_loc)
            for i in range(size):
                h = g * size + i
                outer = edge[h].astype(F32)
                for c in range(chunks):
                    state = (outer + loc[h, c]).astype(BF16)
                    grads[a, h, part(c)] = compute(h, c, state).astype(BF16)
            send(a, g)
            return 0

        lax.fori_loop(begin, end, one, 0)

    def walk_all(way, a, compute, first):
        if first:
            total(way, 0)
        walk(way, a, compute, 0, groups, first)

    def query_part(h, c, state):
        d = dt[h, part(c)]
        adj = masked(d, vt[h, part(c)])
        return (dot(d, state, 1, 1) + dot(adj, kt[h, part(c)], 1, 0)) * fac[part(c)]

    def key_part(h, c, state):
        v = vt[h, part(c)]
        adj = masked_t(v, dt[h, part(c)])
        return dot(v, state, 1, 0) + dot(adj, qt[h, part(c)], 1, 0)

    def value_part(h, c, state):
        k = kt[h, part(c)]
        scores = masked_t(k, qt[h, part(c)])
        return dot(k, state, 1, 1) + dot(scores, dt[h, part(c)], 1, 0)

    @pl.when(lower)
    def _():
        turn(0, 0, True)
        turn(1, 0, True)

    @pl.when(upper)
    def _():
        turn(2, 0, True)
        turn(3, 0, True)

    pl.semaphore_wait(
        barrier, n - 1 + (seq > 0).astype(jnp.int32) + (seq < last).astype(jnp.int32)
    )

    def open_walk(way, a, compute, pair, third):
        for p in range(halves):
            if p:
                for i in pair:
                    turn(i, p)
            total(way, p * half_groups)
            turn(third, p, p == 0)
            walk(way, a, compute, p * half_groups, (p + 1) * half_groups, True)

    def turn_whole(i):
        for p in range(halves):
            turn(i, p, p == 0)

    @pl.when(lower)
    def _():
        open_walk(0, 0, query_part, (0, 1), 2)
        turn_whole(3)
        walk_all(1, 1, key_part, True)
        walk_all(1, 2, value_part, False)

    @pl.when(upper)
    def _():
        open_walk(1, 1, key_part, (2, 3), 1)
        turn_whole(0)
        walk_all(1, 2, value_part, False)
        walk_all(0, 0, query_part, True)

    def attend(g, _):
        for i in range(size):
            h = g * size + i
            before = pre_in[h].astype(F32)
            for c in range(chunks):
                state = (before + kv_loc[h, c]).astype(BF16)
                q = qt[h, part(c)]
                scores = masked(q, kt[h, part(c)])
                out = dot(q, state, 1, 0) + dot(scores, vt[h, part(c)], 1, 0)
                att[h, part(c)] = out.astype(BF16)
        return 0

    lax.fori_loop(0, groups, attend, 0)

    def turn_att(c, _):
        rows = pl.ds(pl.multiple_of(c * block, block), block)
        raw[0, rows] = jnp.swapaxes(att[:, rows, :], 0, 1)
        return 0

    lax.fori_loop(0, tok // block, turn_att, 0)
    att_copy = pltpu.make_async_copy(raw.at[0], att_out, att_sem)
    att_copy.start()

    strip = min(16, tok_out)
    strips = tok_out // strip

    def put(a, slot, r):
        rows = pl.ds(pl.multiple_of(r * strip, strip), strip)
        return pltpu.make_async_copy(
            stage.at[slot, rows], grad_out.at[a, rows], out_sem.at[slot, r]
        )

    def gather(i, _):
        a = lax.rem(i + upper.astype(jnp.int32), 3)
        slot = lax.rem(i, 2)

        @pl.when(i >= 2)
        def _():
            for r in range(strips):
                put(a, slot, r).wait()

        def arrive(g, _):
            own(a, g).wait()
            for off in offsets:
                cross(a, g, off, True).wait_recv()
            return 0

        for p in range(halves):
            lax.fori_loop(p * half_groups, (p + 1) * half_groups, arrive, 0)

            def one(r, _):
                rows = pl.ds(pl.multiple_of(r * strip, strip), strip)
                if halves == 1:
                    x = held[a, :, :, rows, :].reshape(n * heads, strip, dim)
                    stage[slot, rows] = jnp.swapaxes(x, 0, 1)
                else:
                    for src in range(n):
                        x = jnp.swapaxes(held[a, src, some(p), rows, :], 0, 1)
                        stage[slot, rows, pl.ds(src * heads + p * half, half), :] = x
                if p == halves - 1:
                    put(a, slot, r).start()
                return 0

            lax.fori_loop(0, strips, one, 0)
        return 0

    lax.fori_loop(0, 3, gather, 0)

    def drain(g, _):
        @pl.when(seq < last)
        def _():
            chain(0, g).wait_send()

        @pl.when(seq > 0)
        def _():
            chain(1, g).wait_send()

        for a in range(3):
            for off in offsets:
                cross(a, g, off).wait_send()
        return 0

    lax.fori_loop(0, groups, drain, 0)
    for slot in range(2):
        for r in range(strips):
            put(0, slot, r).wait()
    att_copy.wait()


def exchange(nseq, nhead, nsub, queries, key_rows, value_rows, out_adjoint):
    tok, heads, dim = queries.shape
    n = nhead * nsub
    tok_out = tok // n
    chunks = tok // CHUNK
    groups = heads // min(GROUP, heads)
    turned = pltpu.VMEM((heads, tok, dim), BF16)
    low = pltpu.VMEM((heads, dim, dim), BF16)
    any_spec = pl.BlockSpec(memory_space=pl.ANY)
    return pl.pallas_call(
        functools.partial(main_kernel, nseq, nhead, nsub),
        out_shape=(
            pltpu.VMEM((tok, heads, dim), BF16),
            pltpu.VMEM((3, tok_out, n * heads, dim), BF16),
        ),
        in_specs=[any_spec] * 4,
        out_specs=(any_spec,) * 2,
        scratch_shapes=[
            pltpu.VMEM((4, tok, heads, dim), BF16),
            turned, turned, turned, turned,
            pltpu.VMEM((tok, dim), F32),
            pltpu.VMEM((heads, chunks, dim, dim), F32),
            pltpu.VMEM((heads, dim, dim), F32),
            pltpu.VMEM((heads, chunks, dim, dim), F32),
            pltpu.VMEM((heads, dim, dim), F32),
            low, low, low, low,
            pltpu.VMEM((3, heads, tok, dim), BF16),
            pltpu.VMEM((3, n, heads, tok_out, dim), BF16),
            pltpu.VMEM((2, tok_out, n * heads, dim), BF16),
            turned,
            pltpu.SemaphoreType.DMA((4, chunks)),
            pltpu.SemaphoreType.DMA((2, groups)),
            pltpu.SemaphoreType.DMA((2, groups)),
            pltpu.SemaphoreType.DMA((3, groups, n)),
            pltpu.SemaphoreType.DMA((3, groups, n)),
            pltpu.SemaphoreType.DMA((3, groups)),
            pltpu.SemaphoreType.DMA,
            pltpu.SemaphoreType.DMA((2, tok_out // min(16, tok_out))),
        ],
        compiler_params=pltpu.CompilerParams(
            collective_id=0, has_side_effects=True, vmem_limit_bytes=50 * 2**20
        ),
    )(key_rows, value_rows, out_adjoint, queries)


def finish_kernel(pieces, att, grads, att_out, a_out, b_out, c_out, sem):
    outs = (att_out, a_out, b_out, c_out)
    copies = []
    for i, dst in enumerate(outs):
        src = att if i == 0 else grads.at[i - 1]
        step = dst.shape[0] // pieces
        for p in range(pieces):
            rows = pl.ds(p * step, step)
            copies.append(pltpu.make_async_copy(src.at[rows], dst.at[rows], sem.at[i, p]))
    for copy in copies:
        copy.start()
    for copy in copies:
        copy.wait()


def finish(att, grads):
    pieces = 4
    any_spec = pl.BlockSpec(memory_space=pl.ANY)
    return pl.pallas_call(
        functools.partial(finish_kernel, pieces),
        out_shape=(jax.ShapeDtypeStruct(att.shape, BF16),)
        + (jax.ShapeDtypeStruct(grads.shape[1:], BF16),) * 3,
        in_specs=[any_spec] * 2,
        out_specs=(any_spec,) * 4,
        scratch_shapes=[pltpu.SemaphoreType.DMA((4, pieces))],
        compiler_params=pltpu.CompilerParams(vmem_limit_bytes=2**20),
    )(att, grads)


def solution(mesh):
    spec = P(("grp", "seq"), ("head", "sub"), None)
    grad = P(("grp", "seq", "head", "sub"), None, None)

    def per_device(queries, key_rows, value_rows, out_adjoint):
        return finish(
            *exchange(
                mesh.shape["seq"], mesh.shape["head"], mesh.shape["sub"],
                queries, key_rows, value_rows, out_adjoint,
            )
        )

    return jax.shard_map(
        per_device, mesh=mesh, in_specs=(spec,) * 4, out_specs=(spec, grad, grad, grad),
        check_vma=False,
    )
```

```python
import functools

import jax
import jax.numpy as jnp
from jax import lax
from jax.experimental import pallas as pl
from jax.experimental.pallas import tpu as pltpu
from jax.sharding import PartitionSpec as P

MESH = pl.DeviceIdType.MESH
CHUNK = 256
LOAD = 128
GROUP = 2
F32 = jnp.float32
BF16 = jnp.bfloat16


def dot(a, b, da, db):
    return lax.dot_general(a, b, (((da,), (db,)), ((), ())), preferred_element_type=F32)


def main_kernel(
    nseq, nhead, nsub,
    k_hbm, v_hbm, d_hbm, q_hbm,
    att_out, grad_out,
    raw, kt, vt, dt, qt, fac, kv_loc, kv_tot, ad_loc, ad_tot,
    pre_in, pre_out, suf_in, suf_out, grads, held, stage, att,
    in_sem, z_send, z_recv, x_send, x_recv, own_sem, att_sem, out_sem,
):
    heads, tok, dim = kt.shape
    n = nhead * nsub
    tok_out = tok // n
    size = min(GROUP, heads)
    groups = heads // size
    chunks = tok // CHUNK
    seq = lax.axis_index("seq")
    me = lax.axis_index("head") * nsub + lax.axis_index("sub")
    last = nseq - 1
    offsets = sorted(range(1, n), key=lambda o: -min(o, n - o))

    def mate(off):
        other = lax.rem(me + off, n)
        return other, {"head": other // nsub, "sub": lax.rem(other, nsub)}

    barrier = pltpu.get_barrier_semaphore()
    for off in offsets:
        pl.semaphore_signal(barrier, inc=1, device_id=mate(off)[1], device_id_type=MESH)

    @pl.when(seq > 0)
    def _():
        pl.semaphore_signal(barrier, inc=1, device_id={"seq": seq - 1}, device_id_type=MESH)

    @pl.when(seq < last)
    def _():
        pl.semaphore_signal(barrier, inc=1, device_id={"seq": seq + 1}, device_id_type=MESH)

    lower = seq < (nseq + 1) // 2
    upper = jnp.logical_not(lower)
    sources = (k_hbm, v_hbm, d_hbm, q_hbm)

    def load(i, c):
        rows = pl.ds(pl.multiple_of(c * LOAD, LOAD), LOAD)
        return pltpu.make_async_copy(sources[i].at[rows], raw.at[i, rows], in_sem.at[i, c])

    def load_all(order):
        for i in order:
            for c in range(tok // LOAD):
                load(i, c).start()

    @pl.when(lower)
    def _():
        load_all((0, 1, 2, 3))

    @pl.when(upper)
    def _():
        load_all((2, 3, 1, 0))

    row = lax.broadcasted_iota(jnp.int32, (tok, dim), 0)
    fac[...] = lax.rsqrt(F32(dim) * (seq * tok + row + 1).astype(F32))

    @pl.when(seq == 0)
    def _():
        pre_in[...] = jnp.zeros_like(pre_in)

    @pl.when(seq == last)
    def _():
        suf_in[...] = jnp.zeros_like(suf_in)

    block = 64

    halves = 2 if heads % 16 == 0 else 1
    half = heads // halves
    half_groups = groups // halves

    def some(p):
        return pl.ds(p * half, half)

    def turn(i, p, wait=False):
        out = (kt, vt, dt, qt)[i]

        def one(c, _):
            if wait:
                load(i, c).wait()
            for b in range(LOAD // block):
                rows = pl.ds(pl.multiple_of(c * LOAD + b * block, block), block)
                x = jnp.swapaxes(raw[i, rows, some(p), :], 0, 1)
                if i == 3:
                    x = (x.astype(F32) * fac[rows][None]).astype(BF16)
                out[some(p), rows, :] = x
            return 0

        lax.fori_loop(0, tok // LOAD, one, 0)

    def part(c):
        return pl.ds(c * CHUNK, CHUNK)

    def group(g):
        return pl.ds(g * size, size)

    def chain(way, g):
        src, dst, to = (pre_out, pre_in, seq + 1) if way == 0 else (suf_out, suf_in, seq - 1)
        return pltpu.make_async_remote_copy(
            src_ref=src.at[group(g)],
            dst_ref=dst.at[group(g)],
            send_sem=z_send.at[way, g],
            recv_sem=z_recv.at[way, g],
            device_id={"seq": to},
            device_id_type=MESH,
        )

    def ends(way):
        return (seq > 0, seq < last) if way == 0 else (seq < last, seq > 0)

    def total(way, g):
        left, right, loc, tot, out = (
            (kt, vt, kv_loc, kv_tot, pre_out) if way == 0 else (dt, qt, ad_loc, ad_tot, suf_out)
        )
        for i in range(size):
            h = g * size + i
            acc = jnp.zeros((dim, dim), F32)
            for c in range(chunks) if way == 0 else reversed(range(chunks)):
                loc[h, c] = acc
                acc = acc + dot(left[h, part(c)], right[h, part(c)], 0, 0)
            tot[h] = acc
        gets, gives = ends(way)

        @pl.when(jnp.logical_and(jnp.logical_not(gets), gives))
        def _():
            out[group(g)] = tot[group(g)].astype(BF16)
            chain(way, g).start()

    def pass_on(way, g):
        src, dst, tot = (pre_out, pre_in, kv_tot) if way == 0 else (suf_out, suf_in, ad_tot)
        gets, gives = ends(way)

        @pl.when(gets)
        def _():
            chain(way, g).wait_recv()

        @pl.when(jnp.logical_and(gets, gives))
        def _():
            src[group(g)] = (dst[group(g)].astype(F32) + tot[group(g)]).astype(BF16)
            chain(way, g).start()

    def mine(a, g, other):
        rows = pl.ds(pl.multiple_of(other * tok_out, tok_out), tok_out)
        return grads.at[a, group(g), rows]

    def cross(a, g, off, arriving=False):
        other, ids = mate(off)
        src = other if arriving else me
        return pltpu.make_async_remote_copy(
            src_ref=mine(a, g, other),
            dst_ref=held.at[a, src, group(g)],
            send_sem=x_send.at[a, g, other],
            recv_sem=x_recv.at[a, g, src],
            device_id=ids,
            device_id_type=MESH,
        )

    def own(a, g):
        return pltpu.make_async_copy(mine(a, g, me), held.at[a, me, group(g)], own_sem.at[a, g])

    def send(a, g):
        for off in offsets:
            cross(a, g, off).start()
        own(a, g).start()

    across = lax.broadcasted_iota(jnp.int32, (CHUNK, CHUNK), 0)
    along = lax.broadcasted_iota(jnp.int32, (CHUNK, CHUNK), 1)

    def masked(a, b):
        return jnp.where(across >= along, dot(a, b, 1, 1), 0.0).astype(BF16)

    def masked_t(a, b):
        return jnp.where(across <= along, dot(a, b, 1, 1), 0.0).astype(BF16)

    def walk(way, a, compute, begin, end, first):
        def one(g, _):
            if first:
                @pl.when(g + 1 < end)
                def _():
                    total(way, g + 1)

                pass_on(way, g)
            edge, loc = (pre_in, kv_loc) if way == 0 else (suf_in, ad_loc)
            for i in range(size):
                h = g * size + i
                outer = edge[h].astype(F32)
                for c in range(chunks):
                    state = (outer + loc[h, c]).astype(BF16)
                    grads[a, h, part(c)] = compute(h, c, state).astype(BF16)
            send(a, g)
            return 0

        lax.fori_loop(begin, end, one, 0)

    def walk_all(way, a, compute, first):
        if first:
            total(way, 0)
        walk(way, a, compute, 0, groups, first)

    def query_part(h, c, state):
        d = dt[h, part(c)]
        adj = masked(d, vt[h, part(c)])
        return (dot(d, state, 1, 1) + dot(adj, kt[h, part(c)], 1, 0)) * fac[part(c)]

    def key_part(h, c, state):
        v = vt[h, part(c)]
        adj = masked_t(v, dt[h, part(c)])
        return dot(v, state, 1, 0) + dot(adj, qt[h, part(c)], 1, 0)

    def value_part(h, c, state):
        k = kt[h, part(c)]
        scores = masked_t(k, qt[h, part(c)])
        return dot(k, state, 1, 1) + dot(scores, dt[h, part(c)], 1, 0)

    @pl.when(lower)
    def _():
        turn(0, 0, True)
        turn(1, 0, True)

    @pl.when(upper)
    def _():
        turn(2, 0, True)
        turn(3, 0, True)

    pl.semaphore_wait(
        barrier, n - 1 + (seq > 0).astype(jnp.int32) + (seq < last).astype(jnp.int32)
    )

    def open_walk(way, a, compute, pair, third):
        for p in range(halves):
            if p:
                for i in pair:
                    turn(i, p)
            total(way, p * half_groups)
            turn(third, p, p == 0)
            walk(way, a, compute, p * half_groups, (p + 1) * half_groups, True)

    def turn_whole(i):
        for p in range(halves):
            turn(i, p, p == 0)

    @pl.when(lower)
    def _():
        open_walk(0, 0, query_part, (0, 1), 2)
        turn_whole(3)
        walk_all(1, 1, key_part, True)
        walk_all(1, 2, value_part, False)

    @pl.when(upper)
    def _():
        open_walk(1, 1, key_part, (2, 3), 1)
        turn_whole(0)
        walk_all(1, 2, value_part, False)
        walk_all(0, 0, query_part, True)

    def attend(g, _):
        for i in range(size):
            h = g * size + i
            before = pre_in[h].astype(F32)
            for c in range(chunks):
                state = (before + kv_loc[h, c]).astype(BF16)
                q = qt[h, part(c)]
                scores = masked(q, kt[h, part(c)])
                out = dot(q, state, 1, 0) + dot(scores, vt[h, part(c)], 1, 0)
                att[h, part(c)] = out.astype(BF16)
        return 0

    lax.fori_loop(0, groups, attend, 0)

    def turn_att(c, _):
        rows = pl.ds(pl.multiple_of(c * block, block), block)
        raw[0, rows] = jnp.swapaxes(att[:, rows, :], 0, 1)
        return 0

    lax.fori_loop(0, tok // block, turn_att, 0)
    att_copy = pltpu.make_async_copy(raw.at[0], att_out, att_sem)
    att_copy.start()

    strip = min(16, tok_out)
    strips = tok_out // strip

    def put(a, slot, r):
        rows = pl.ds(pl.multiple_of(r * strip, strip), strip)
        return pltpu.make_async_copy(
            stage.at[slot, rows], grad_out.at[a, rows], out_sem.at[slot, r]
        )

    def gather(i, _):
        a = lax.rem(i + upper.astype(jnp.int32), 3)
        slot = lax.rem(i, 2)

        @pl.when(i >= 2)
        def _():
            for r in range(strips):
                put(a, slot, r).wait()

        def arrive(g, _):
            own(a, g).wait()
            for off in offsets:
                cross(a, g, off, True).wait_recv()
            return 0

        for p in range(halves):
            lax.fori_loop(p * half_groups, (p + 1) * half_groups, arrive, 0)

            def one(r, _):
                rows = pl.ds(pl.multiple_of(r * strip, strip), strip)
                if halves == 1:
                    x = held[a, :, :, rows, :].reshape(n * heads, strip, dim)
                    stage[slot, rows] = jnp.swapaxes(x, 0, 1)
                else:
                    for src in range(n):
                        x = jnp.swapaxes(held[a, src, some(p), rows, :], 0, 1)
                        stage[slot, rows, pl.ds(src * heads + p * half, half), :] = x
                if p == halves - 1:
                    put(a, slot, r).start()
                return 0

            lax.fori_loop(0, strips, one, 0)
        return 0

    lax.fori_loop(0, 3, gather, 0)

    def drain(g, _):
        @pl.when(seq < last)
        def _():
            chain(0, g).wait_send()

        @pl.when(seq > 0)
        def _():
            chain(1, g).wait_send()

        for a in range(3):
            for off in offsets:
                cross(a, g, off).wait_send()
        return 0

    lax.fori_loop(0, groups, drain, 0)
    for slot in range(2):
        for r in range(strips):
            put(0, slot, r).wait()
    att_copy.wait()


def exchange(nseq, nhead, nsub, queries, key_rows, value_rows, out_adjoint):
    tok, heads, dim = queries.shape
    n = nhead * nsub
    tok_out = tok // n
    chunks = tok // CHUNK
    groups = heads // min(GROUP, heads)
    turned = pltpu.VMEM((heads, tok, dim), BF16)
    low = pltpu.VMEM((heads, dim, dim), BF16)
    any_spec = pl.BlockSpec(memory_space=pl.ANY)
    return pl.pallas_call(
        functools.partial(main_kernel, nseq, nhead, nsub),
        out_shape=(
            pltpu.VMEM((tok, heads, dim), BF16),
            pltpu.VMEM((3, tok_out, n * heads, dim), BF16),
        ),
        in_specs=[any_spec] * 4,
        out_specs=(any_spec,) * 2,
        scratch_shapes=[
            pltpu.VMEM((4, tok, heads, dim), BF16),
            turned, turned, turned, turned,
            pltpu.VMEM((tok, dim), F32),
            pltpu.VMEM((heads, chunks, dim, dim), F32),
            pltpu.VMEM((heads, dim, dim), F32),
            pltpu.VMEM((heads, chunks, dim, dim), F32),
            pltpu.VMEM((heads, dim, dim), F32),
            low, low, low, low,
            pltpu.VMEM((3, heads, tok, dim), BF16),
            pltpu.VMEM((3, n, heads, tok_out, dim), BF16),
            pltpu.VMEM((2, tok_out, n * heads, dim), BF16),
            turned,
            pltpu.SemaphoreType.DMA((4, tok // LOAD)),
            pltpu.SemaphoreType.DMA((2, groups)),
            pltpu.SemaphoreType.DMA((2, groups)),
            pltpu.SemaphoreType.DMA((3, groups, n)),
            pltpu.SemaphoreType.DMA((3, groups, n)),
            pltpu.SemaphoreType.DMA((3, groups)),
            pltpu.SemaphoreType.DMA,
            pltpu.SemaphoreType.DMA((2, tok_out // min(16, tok_out))),
        ],
        compiler_params=pltpu.CompilerParams(
            collective_id=0, has_side_effects=True, vmem_limit_bytes=50 * 2**20
        ),
    )(key_rows, value_rows, out_adjoint, queries)


def finish_kernel(pieces, att, grads, att_out, a_out, b_out, c_out, sem):
    outs = (att_out, a_out, b_out, c_out)
    copies = []
    for i, dst in enumerate(outs):
        src = att if i == 0 else grads.at[i - 1]
        step = dst.shape[0] // pieces
        for p in range(pieces):
            rows = pl.ds(p * step, step)
            copies.append(pltpu.make_async_copy(src.at[rows], dst.at[rows], sem.at[i, p]))
    for copy in copies:
        copy.start()
    for copy in copies:
        copy.wait()


def finish(att, grads):
    pieces = 4
    any_spec = pl.BlockSpec(memory_space=pl.ANY)
    return pl.pallas_call(
        functools.partial(finish_kernel, pieces),
        out_shape=(jax.ShapeDtypeStruct(att.shape, BF16),)
        + (jax.ShapeDtypeStruct(grads.shape[1:], BF16),) * 3,
        in_specs=[any_spec] * 2,
        out_specs=(any_spec,) * 4,
        scratch_shapes=[pltpu.SemaphoreType.DMA((4, pieces))],
        compiler_params=pltpu.CompilerParams(vmem_limit_bytes=2**20),
    )(att, grads)


def solution(mesh):
    spec = P(("grp", "seq"), ("head", "sub"), None)
    grad = P(("grp", "seq", "head", "sub"), None, None)

    def per_device(queries, key_rows, value_rows, out_adjoint):
        return finish(
            *exchange(
                mesh.shape["seq"], mesh.shape["head"], mesh.shape["sub"],
                queries, key_rows, value_rows, out_adjoint,
            )
        )

    return jax.shard_map(
        per_device, mesh=mesh, in_specs=(spec,) * 4, out_specs=(spec, grad, grad, grad),
        check_vma=False,
    )
```

```python
import functools

import jax
import jax.numpy as jnp
from jax import lax
from jax.experimental import pallas as pl
from jax.experimental.pallas import tpu as pltpu
from jax.sharding import PartitionSpec as P

MESH = pl.DeviceIdType.MESH
CHUNK = 128
GROUP = 2
F32 = jnp.float32
BF16 = jnp.bfloat16


def dot(a, b, da, db):
    return lax.dot_general(a, b, (((da,), (db,)), ((), ())), preferred_element_type=F32)


def main_kernel(
    nseq, nhead, nsub,
    k_hbm, v_hbm, d_hbm, q_hbm,
    att_out, grad_out,
    raw, kt, vt, dt, qt, fac, kv_loc, kv_tot, ad_loc, ad_tot,
    pre_in, pre_out, suf_in, suf_out, grads, held, stage, att,
    in_sem, z_send, z_recv, x_send, x_recv, own_sem, att_sem, out_sem,
):
    heads, tok, dim = kt.shape
    n = nhead * nsub
    tok_out = tok // n
    size = min(GROUP, heads)
    groups = heads // size
    chunks = tok // CHUNK
    seq = lax.axis_index("seq")
    me = lax.axis_index("head") * nsub + lax.axis_index("sub")
    last = nseq - 1
    offsets = sorted(range(1, n), key=lambda o: -min(o, n - o))

    def mate(off):
        other = lax.rem(me + off, n)
        return other, {"head": other // nsub, "sub": lax.rem(other, nsub)}

    barrier = pltpu.get_barrier_semaphore()
    for off in offsets:
        pl.semaphore_signal(barrier, inc=1, device_id=mate(off)[1], device_id_type=MESH)

    @pl.when(seq > 0)
    def _():
        pl.semaphore_signal(barrier, inc=1, device_id={"seq": seq - 1}, device_id_type=MESH)

    @pl.when(seq < last)
    def _():
        pl.semaphore_signal(barrier, inc=1, device_id={"seq": seq + 1}, device_id_type=MESH)

    lower = seq < (nseq + 1) // 2
    upper = jnp.logical_not(lower)
    sources = (k_hbm, v_hbm, d_hbm, q_hbm)

    def load(i, c):
        rows = pl.ds(pl.multiple_of(c * CHUNK, CHUNK), CHUNK)
        return pltpu.make_async_copy(sources[i].at[rows], raw.at[i, rows], in_sem.at[i, c])

    def load_all(order):
        for i in order:
            for c in range(chunks):
                load(i, c).start()

    @pl.when(lower)
    def _():
        load_all((0, 1))

    @pl.when(upper)
    def _():
        load_all((2, 3))

    row = lax.broadcasted_iota(jnp.int32, (tok, dim), 0)
    fac[...] = lax.rsqrt(F32(dim) * (seq * tok + row + 1).astype(F32))

    @pl.when(seq == 0)
    def _():
        pre_in[...] = jnp.zeros_like(pre_in)

    @pl.when(seq == last)
    def _():
        suf_in[...] = jnp.zeros_like(suf_in)

    block = 64

    halves = 2 if heads % 16 == 0 else 1
    half = heads // halves
    half_groups = groups // halves

    def some(p):
        return pl.ds(p * half, half)

    def turn(i, p, wait=False):
        out = (kt, vt, dt, qt)[i]

        def one(c, _):
            if wait:
                load(i, c).wait()
            for b in range(CHUNK // block):
                rows = pl.ds(pl.multiple_of(c * CHUNK + b * block, block), block)
                x = jnp.swapaxes(raw[i, rows, some(p), :], 0, 1)
                if i == 3:
                    x = (x.astype(F32) * fac[rows][None]).astype(BF16)
                out[some(p), rows, :] = x
            return 0

        lax.fori_loop(0, chunks, one, 0)

    def part(c):
        return pl.ds(c * CHUNK, CHUNK)

    def group(g):
        return pl.ds(g * size, size)

    def chain(way, g):
        src, dst, to = (pre_out, pre_in, seq + 1) if way == 0 else (suf_out, suf_in, seq - 1)
        return pltpu.make_async_remote_copy(
            src_ref=src.at[group(g)],
            dst_ref=dst.at[group(g)],
            send_sem=z_send.at[way, g],
            recv_sem=z_recv.at[way, g],
            device_id={"seq": to},
            device_id_type=MESH,
        )

    def ends(way):
        return (seq > 0, seq < last) if way == 0 else (seq < last, seq > 0)

    def total(way, g):
        left, right, loc, tot, out = (
            (kt, vt, kv_loc, kv_tot, pre_out) if way == 0 else (dt, qt, ad_loc, ad_tot, suf_out)
        )
        for i in range(size):
            h = g * size + i
            acc = jnp.zeros((dim, dim), F32)
            for c in range(chunks) if way == 0 else reversed(range(chunks)):
                loc[h, c] = acc
                acc = acc + dot(left[h, part(c)], right[h, part(c)], 0, 0)
            tot[h] = acc
        gets, gives = ends(way)

        @pl.when(jnp.logical_and(jnp.logical_not(gets), gives))
        def _():
            out[group(g)] = tot[group(g)].astype(BF16)
            chain(way, g).start()

    def pass_on(way, g):
        src, dst, tot = (pre_out, pre_in, kv_tot) if way == 0 else (suf_out, suf_in, ad_tot)
        gets, gives = ends(way)

        @pl.when(gets)
        def _():
            chain(way, g).wait_recv()

        @pl.when(jnp.logical_and(gets, gives))
        def _():
            src[group(g)] = (dst[group(g)].astype(F32) + tot[group(g)]).astype(BF16)
            chain(way, g).start()

    def mine(a, g, other):
        rows = pl.ds(pl.multiple_of(other * tok_out, tok_out), tok_out)
        return grads.at[a, group(g), rows]

    def cross(a, g, off, arriving=False):
        other, ids = mate(off)
        src = other if arriving else me
        return pltpu.make_async_remote_copy(
            src_ref=mine(a, g, other),
            dst_ref=held.at[a, src, group(g)],
            send_sem=x_send.at[a, g, other],
            recv_sem=x_recv.at[a, g, src],
            device_id=ids,
            device_id_type=MESH,
        )

    def own(a, g):
        return pltpu.make_async_copy(mine(a, g, me), held.at[a, me, group(g)], own_sem.at[a, g])

    def send(a, g):
        for off in offsets:
            cross(a, g, off).start()
        own(a, g).start()

    across = lax.broadcasted_iota(jnp.int32, (CHUNK, CHUNK), 0)
    along = lax.broadcasted_iota(jnp.int32, (CHUNK, CHUNK), 1)

    def masked(a, b):
        return jnp.where(across >= along, dot(a, b, 1, 1), 0.0).astype(BF16)

    def masked_t(a, b):
        return jnp.where(across <= along, dot(a, b, 1, 1), 0.0).astype(BF16)

    def walk(way, a, compute, begin, end, first):
        def one(g, _):
            if first:
                pass_on(way, g)
            edge, loc = (pre_in, kv_loc) if way == 0 else (suf_in, ad_loc)
            for i in range(size):
                h = g * size + i
                outer = edge[h].astype(F32)
                for c in range(chunks):
                    state = (outer + loc[h, c]).astype(BF16)
                    grads[a, h, part(c)] = compute(h, c, state).astype(BF16)
            send(a, g)
            if first:
                @pl.when(g + 1 < end)
                def _():
                    total(way, g + 1)

            return 0

        lax.fori_loop(begin, end, one, 0)

    def walk_all(way, a, compute, first):
        if first:
            total(way, 0)
        walk(way, a, compute, 0, groups, first)

    def query_part(h, c, state):
        d = dt[h, part(c)]
        adj = masked(d, vt[h, part(c)])
        return (dot(d, state, 1, 1) + dot(adj, kt[h, part(c)], 1, 0)) * fac[part(c)]

    def key_part(h, c, state):
        v = vt[h, part(c)]
        adj = masked_t(v, dt[h, part(c)])
        return dot(v, state, 1, 0) + dot(adj, qt[h, part(c)], 1, 0)

    def value_part(h, c, state):
        k = kt[h, part(c)]
        scores = masked_t(k, qt[h, part(c)])
        return dot(k, state, 1, 1) + dot(scores, dt[h, part(c)], 1, 0)

    @pl.when(lower)
    def _():
        turn(0, 0, True)
        load_all((2,))
        turn(1, 0, True)
        load_all((3,))

    @pl.when(upper)
    def _():
        turn(2, 0, True)
        load_all((1,))
        turn(3, 0, True)
        load_all((0,))

    pl.semaphore_wait(
        barrier, n - 1 + (seq > 0).astype(jnp.int32) + (seq < last).astype(jnp.int32)
    )

    def open_walk(way, a, compute, pair, third):
        for p in range(halves):
            if p:
                for i in pair:
                    turn(i, p)
            total(way, p * half_groups)
            turn(third, p, p == 0)
            walk(way, a, compute, p * half_groups, (p + 1) * half_groups, True)

    def turn_whole(i):
        for p in range(halves):
            turn(i, p, p == 0)

    @pl.when(lower)
    def _():
        open_walk(0, 0, query_part, (0, 1), 2)
        turn_whole(3)
        walk_all(1, 1, key_part, True)
        walk_all(1, 2, value_part, False)

    @pl.when(upper)
    def _():
        open_walk(1, 1, key_part, (2, 3), 1)
        turn_whole(0)
        walk_all(1, 2, value_part, False)
        walk_all(0, 0, query_part, True)

    def attend(g, _):
        for i in range(size):
            h = g * size + i
            before = pre_in[h].astype(F32)
            for c in range(chunks):
                state = (before + kv_loc[h, c]).astype(BF16)
                q = qt[h, part(c)]
                scores = masked(q, kt[h, part(c)])
                out = dot(q, state, 1, 0) + dot(scores, vt[h, part(c)], 1, 0)
                att[h, part(c)] = out.astype(BF16)
        return 0

    lax.fori_loop(0, groups, attend, 0)

    def turn_att(c, _):
        rows = pl.ds(pl.multiple_of(c * block, block), block)
        raw[0, rows] = jnp.swapaxes(att[:, rows, :], 0, 1)
        return 0

    lax.fori_loop(0, tok // block, turn_att, 0)
    att_copy = pltpu.make_async_copy(raw.at[0], att_out, att_sem)
    att_copy.start()

    strip = min(16, tok_out)
    strips = tok_out // strip

    def put(a, slot, r):
        rows = pl.ds(pl.multiple_of(r * strip, strip), strip)
        return pltpu.make_async_copy(
            stage.at[slot, rows], grad_out.at[a, rows], out_sem.at[slot, r]
        )

    def gather(i, _):
        a = lax.rem(i + upper.astype(jnp.int32), 3)
        slot = lax.rem(i, 2)

        @pl.when(i >= 2)
        def _():
            for r in range(strips):
                put(a, slot, r).wait()

        def arrive(g, _):
            own(a, g).wait()
            for off in offsets:
                cross(a, g, off, True).wait_recv()
            return 0

        for p in range(halves):
            lax.fori_loop(p * half_groups, (p + 1) * half_groups, arrive, 0)

            def one(r, _):
                rows = pl.ds(pl.multiple_of(r * strip, strip), strip)
                if halves == 1:
                    x = held[a, :, :, rows, :].reshape(n * heads, strip, dim)
                    stage[slot, rows] = jnp.swapaxes(x, 0, 1)
                else:
                    for src in range(n):
                        x = jnp.swapaxes(held[a, src, some(p), rows, :], 0, 1)
                        stage[slot, rows, pl.ds(src * heads + p * half, half), :] = x
                if p == halves - 1:
                    put(a, slot, r).start()
                return 0

            lax.fori_loop(0, strips, one, 0)
        return 0

    lax.fori_loop(0, 3, gather, 0)

    def drain(g, _):
        @pl.when(seq < last)
        def _():
            chain(0, g).wait_send()

        @pl.when(seq > 0)
        def _():
            chain(1, g).wait_send()

        for a in range(3):
            for off in offsets:
                cross(a, g, off).wait_send()
        return 0

    lax.fori_loop(0, groups, drain, 0)
    for slot in range(2):
        for r in range(strips):
            put(0, slot, r).wait()
    att_copy.wait()


def exchange(nseq, nhead, nsub, queries, key_rows, value_rows, out_adjoint):
    tok, heads, dim = queries.shape
    n = nhead * nsub
    tok_out = tok // n
    chunks = tok // CHUNK
    groups = heads // min(GROUP, heads)
    turned = pltpu.VMEM((heads, tok, dim), BF16)
    low = pltpu.VMEM((heads, dim, dim), BF16)
    any_spec = pl.BlockSpec(memory_space=pl.ANY)
    return pl.pallas_call(
        functools.partial(main_kernel, nseq, nhead, nsub),
        out_shape=(
            pltpu.VMEM((tok, heads, dim), BF16),
            pltpu.VMEM((3, tok_out, n * heads, dim), BF16),
        ),
        in_specs=[any_spec] * 4,
        out_specs=(any_spec,) * 2,
        scratch_shapes=[
            pltpu.VMEM((4, tok, heads, dim), BF16),
            turned, turned, turned, turned,
            pltpu.VMEM((tok, dim), F32),
            pltpu.VMEM((heads, chunks, dim, dim), F32),
            pltpu.VMEM((heads, dim, dim), F32),
            pltpu.VMEM((heads, chunks, dim, dim), F32),
            pltpu.VMEM((heads, dim, dim), F32),
            low, low, low, low,
            pltpu.VMEM((3, heads, tok, dim), BF16),
            pltpu.VMEM((3, n, heads, tok_out, dim), BF16),
            pltpu.VMEM((2, tok_out, n * heads, dim), BF16),
            turned,
            pltpu.SemaphoreType.DMA((4, chunks)),
            pltpu.SemaphoreType.DMA((2, groups)),
            pltpu.SemaphoreType.DMA((2, groups)),
            pltpu.SemaphoreType.DMA((3, groups, n)),
            pltpu.SemaphoreType.DMA((3, groups, n)),
            pltpu.SemaphoreType.DMA((3, groups)),
            pltpu.SemaphoreType.DMA,
            pltpu.SemaphoreType.DMA((2, tok_out // min(16, tok_out))),
        ],
        compiler_params=pltpu.CompilerParams(
            collective_id=0, has_side_effects=True, vmem_limit_bytes=50 * 2**20
        ),
    )(key_rows, value_rows, out_adjoint, queries)


def finish_kernel(pieces, att, grads, att_out, a_out, b_out, c_out, sem):
    outs = (att_out, a_out, b_out, c_out)
    copies = []
    for i, dst in enumerate(outs):
        src = att if i == 0 else grads.at[i - 1]
        step = dst.shape[0] // pieces
        for p in range(pieces):
            rows = pl.ds(p * step, step)
            copies.append(pltpu.make_async_copy(src.at[rows], dst.at[rows], sem.at[i, p]))
    for copy in copies:
        copy.start()
    for copy in copies:
        copy.wait()


def finish(att, grads):
    pieces = 4
    any_spec = pl.BlockSpec(memory_space=pl.ANY)
    return pl.pallas_call(
        functools.partial(finish_kernel, pieces),
        out_shape=(jax.ShapeDtypeStruct(att.shape, BF16),)
        + (jax.ShapeDtypeStruct(grads.shape[1:], BF16),) * 3,
        in_specs=[any_spec] * 2,
        out_specs=(any_spec,) * 4,
        scratch_shapes=[pltpu.SemaphoreType.DMA((4, pieces))],
        compiler_params=pltpu.CompilerParams(vmem_limit_bytes=2**20),
    )(att, grads)


def solution(mesh):
    spec = P(("grp", "seq"), ("head", "sub"), None)
    grad = P(("grp", "seq", "head", "sub"), None, None)

    def per_device(queries, key_rows, value_rows, out_adjoint):
        return finish(
            *exchange(
                mesh.shape["seq"], mesh.shape["head"], mesh.shape["sub"],
                queries, key_rows, value_rows, out_adjoint,
            )
        )

    return jax.shard_map(
        per_device, mesh=mesh, in_specs=(spec,) * 4, out_specs=(spec, grad, grad, grad),
        check_vma=False,
    )
```

```python
import functools

import jax
import jax.numpy as jnp
from jax import lax
from jax.experimental import pallas as pl
from jax.experimental.pallas import tpu as pltpu
from jax.sharding import PartitionSpec as P

MESH = pl.DeviceIdType.MESH
CHUNK = 128
GROUP = 2
F32 = jnp.float32
BF16 = jnp.bfloat16


def dot(a, b, da, db):
    return lax.dot_general(a, b, (((da,), (db,)), ((), ())), preferred_element_type=F32)


def main_kernel(
    nseq, nhead, nsub,
    k_hbm, v_hbm, d_hbm, q_hbm,
    att_out, grad_out, final,
    raw, kt, vt, dt, qt, fac, kv_loc, kv_tot, ad_loc, ad_tot,
    pre_in, pre_out, suf_in, suf_out, grads, held, stage, att,
    in_sem, z_send, z_recv, x_send, x_recv, own_sem, att_sem, out_sem,
):
    heads, tok, dim = kt.shape
    n = nhead * nsub
    tok_out = tok // n
    size = min(GROUP, heads)
    groups = heads // size
    chunks = tok // CHUNK
    seq = lax.axis_index("seq")
    me = lax.axis_index("head") * nsub + lax.axis_index("sub")
    last = nseq - 1
    offsets = sorted(range(1, n), key=lambda o: -min(o, n - o))

    def mate(off):
        other = lax.rem(me + off, n)
        return other, {"head": other // nsub, "sub": lax.rem(other, nsub)}

    barrier = pltpu.get_barrier_semaphore()
    for off in offsets:
        pl.semaphore_signal(barrier, inc=1, device_id=mate(off)[1], device_id_type=MESH)

    @pl.when(seq > 0)
    def _():
        pl.semaphore_signal(barrier, inc=1, device_id={"seq": seq - 1}, device_id_type=MESH)

    @pl.when(seq < last)
    def _():
        pl.semaphore_signal(barrier, inc=1, device_id={"seq": seq + 1}, device_id_type=MESH)

    lower = seq < (nseq + 1) // 2
    upper = jnp.logical_not(lower)
    sources = (k_hbm, v_hbm, d_hbm, q_hbm)

    def load(i, c):
        rows = pl.ds(pl.multiple_of(c * CHUNK, CHUNK), CHUNK)
        return pltpu.make_async_copy(sources[i].at[rows], raw.at[i, rows], in_sem.at[i, c])

    def load_all(order):
        for i in order:
            for c in range(chunks):
                load(i, c).start()

    @pl.when(lower)
    def _():
        load_all((0, 1, 2, 3))

    @pl.when(upper)
    def _():
        load_all((2, 3, 1, 0))

    row = lax.broadcasted_iota(jnp.int32, (tok, dim), 0)
    fac[...] = lax.rsqrt(F32(dim) * (seq * tok + row + 1).astype(F32))

    @pl.when(seq == 0)
    def _():
        pre_in[...] = jnp.zeros_like(pre_in)

    @pl.when(seq == last)
    def _():
        suf_in[...] = jnp.zeros_like(suf_in)

    block = 64

    halves = 2 if heads % 16 == 0 else 1
    half = heads // halves
    half_groups = groups // halves

    def some(p):
        return pl.ds(p * half, half)

    def turn(i, p, wait=False):
        out = (kt, vt, dt, qt)[i]

        def one(c, _):
            if wait:
                load(i, c).wait()
            for b in range(CHUNK // block):
                rows = pl.ds(pl.multiple_of(c * CHUNK + b * block, block), block)
                x = jnp.swapaxes(raw[i, rows, some(p), :], 0, 1)
                if i == 3:
                    x = (x.astype(F32) * fac[rows][None]).astype(BF16)
                out[some(p), rows, :] = x
            return 0

        lax.fori_loop(0, chunks, one, 0)

    def part(c):
        return pl.ds(c * CHUNK, CHUNK)

    def group(g):
        return pl.ds(g * size, size)

    def chain(way, g):
        src, dst, to = (pre_out, pre_in, seq + 1) if way == 0 else (suf_out, suf_in, seq - 1)
        return pltpu.make_async_remote_copy(
            src_ref=src.at[group(g)],
            dst_ref=dst.at[group(g)],
            send_sem=z_send.at[way, g],
            recv_sem=z_recv.at[way, g],
            device_id={"seq": to},
            device_id_type=MESH,
        )

    def ends(way):
        return (seq > 0, seq < last) if way == 0 else (seq < last, seq > 0)

    def total(way, g):
        left, right, loc, tot, out = (
            (kt, vt, kv_loc, kv_tot, pre_out) if way == 0 else (dt, qt, ad_loc, ad_tot, suf_out)
        )
        for i in range(size):
            h = g * size + i
            acc = jnp.zeros((dim, dim), F32)
            for c in range(chunks) if way == 0 else reversed(range(chunks)):
                loc[h, c] = acc
                acc = acc + dot(left[h, part(c)], right[h, part(c)], 0, 0)
            tot[h] = acc
        gets, gives = ends(way)

        @pl.when(jnp.logical_and(jnp.logical_not(gets), gives))
        def _():
            out[group(g)] = tot[group(g)].astype(BF16)
            chain(way, g).start()

    def pass_on(way, g):
        src, dst, tot = (pre_out, pre_in, kv_tot) if way == 0 else (suf_out, suf_in, ad_tot)
        gets, gives = ends(way)

        @pl.when(gets)
        def _():
            chain(way, g).wait_recv()

        @pl.when(jnp.logical_and(gets, gives))
        def _():
            src[group(g)] = (dst[group(g)].astype(F32) + tot[group(g)]).astype(BF16)
            chain(way, g).start()

    def mine(a, g, other):
        rows = pl.ds(pl.multiple_of(other * tok_out, tok_out), tok_out)
        return grads.at[a, group(g), rows]

    def landing(a, src, g):
        return held.at[a, src, group(g)] if a < 2 else final.at[src, group(g)]

    def cross(a, g, off, arriving=False):
        other, ids = mate(off)
        src = other if arriving else me
        return pltpu.make_async_remote_copy(
            src_ref=mine(a, g, other),
            dst_ref=landing(a, src, g),
            send_sem=x_send.at[a, g, other],
            recv_sem=x_recv.at[a, g, src],
            device_id=ids,
            device_id_type=MESH,
        )

    def own(a, g):
        return pltpu.make_async_copy(mine(a, g, me), landing(a, me, g), own_sem.at[a, g])

    def send(a, g):
        for off in offsets:
            cross(a, g, off).start()
        own(a, g).start()

    across = lax.broadcasted_iota(jnp.int32, (CHUNK, CHUNK), 0)
    along = lax.broadcasted_iota(jnp.int32, (CHUNK, CHUNK), 1)

    def masked(a, b):
        return jnp.where(across >= along, dot(a, b, 1, 1), 0.0).astype(BF16)

    def masked_t(a, b):
        return jnp.where(across <= along, dot(a, b, 1, 1), 0.0).astype(BF16)

    def walk(way, a, compute, begin, end, first):
        def one(g, _):
            if first:
                @pl.when(g + 1 < end)
                def _():
                    total(way, g + 1)

                pass_on(way, g)
            edge, loc = (pre_in, kv_loc) if way == 0 else (suf_in, ad_loc)
            for i in range(size):
                h = g * size + i
                outer = edge[h].astype(F32)
                for c in range(chunks):
                    state = (outer + loc[h, c]).astype(BF16)
                    grads[a, h, part(c)] = compute(h, c, state).astype(BF16)
            send(a, g)
            return 0

        lax.fori_loop(begin, end, one, 0)

    def walk_all(way, a, compute, first):
        if first:
            total(way, 0)
        walk(way, a, compute, 0, groups, first)

    def query_part(h, c, state):
        d = dt[h, part(c)]
        adj = masked(d, vt[h, part(c)])
        return (dot(d, state, 1, 1) + dot(adj, kt[h, part(c)], 1, 0)) * fac[part(c)]

    def key_part(h, c, state):
        v = vt[h, part(c)]
        adj = masked_t(v, dt[h, part(c)])
        return dot(v, state, 1, 0) + dot(adj, qt[h, part(c)], 1, 0)

    def value_part(h, c, state):
        k = kt[h, part(c)]
        scores = masked_t(k, qt[h, part(c)])
        return dot(k, state, 1, 1) + dot(scores, dt[h, part(c)], 1, 0)

    @pl.when(lower)
    def _():
        turn(0, 0, True)
        turn(1, 0, True)

    @pl.when(upper)
    def _():
        turn(2, 0, True)
        turn(3, 0, True)

    pl.semaphore_wait(
        barrier, n - 1 + (seq > 0).astype(jnp.int32) + (seq < last).astype(jnp.int32)
    )

    def open_walk(way, a, compute, pair, third):
        for p in range(halves):
            if p:
                for i in pair:
                    turn(i, p)
            total(way, p * half_groups)
            turn(third, p, p == 0)
            walk(way, a, compute, p * half_groups, (p + 1) * half_groups, True)

    def turn_whole(i):
        for p in range(halves):
            turn(i, p, p == 0)

    @pl.when(lower)
    def _():
        open_walk(0, 0, query_part, (0, 1), 2)
        turn_whole(3)
        walk_all(1, 1, key_part, True)
        walk_all(1, 2, value_part, False)

    @pl.when(upper)
    def _():
        open_walk(1, 0, key_part, (2, 3), 1)
        turn_whole(0)
        walk_all(1, 1, value_part, False)
        walk_all(0, 2, query_part, True)

    def attend(g, _):
        for i in range(size):
            h = g * size + i
            before = pre_in[h].astype(F32)
            for c in range(chunks):
                state = (before + kv_loc[h, c]).astype(BF16)
                q = qt[h, part(c)]
                scores = masked(q, kt[h, part(c)])
                out = dot(q, state, 1, 0) + dot(scores, vt[h, part(c)], 1, 0)
                att[h, part(c)] = out.astype(BF16)
        return 0

    lax.fori_loop(0, groups, attend, 0)

    def turn_att(c, _):
        rows = pl.ds(pl.multiple_of(c * block, block), block)
        raw[0, rows] = jnp.swapaxes(att[:, rows, :], 0, 1)
        return 0

    lax.fori_loop(0, tok // block, turn_att, 0)
    att_copy = pltpu.make_async_copy(raw.at[0], att_out, att_sem)
    att_copy.start()

    strip = min(16, tok_out)
    strips = tok_out // strip

    def put(slot, r):
        rows = pl.ds(pl.multiple_of(r * strip, strip), strip)
        return pltpu.make_async_copy(
            stage.at[slot, rows], grad_out.at[slot, rows], out_sem.at[slot, r]
        )

    for a in range(3):
        def arrive(g, _):
            own(a, g).wait()
            for off in offsets:
                cross(a, g, off, True).wait_recv()
            return 0

        def one(p, r, _):
            rows = pl.ds(pl.multiple_of(r * strip, strip), strip)
            if halves == 1:
                x = held[a, :, :, rows, :].reshape(n * heads, strip, dim)
                stage[a, rows] = jnp.swapaxes(x, 0, 1)
            else:
                for src in range(n):
                    x = jnp.swapaxes(held[a, src, some(p), rows, :], 0, 1)
                    stage[a, rows, pl.ds(src * heads + p * half, half), :] = x
            if p == halves - 1:
                put(a, r).start()
            return 0

        for p in range(halves):
            lax.fori_loop(p * half_groups, (p + 1) * half_groups, arrive, 0)
            if a < 2:
                lax.fori_loop(0, strips, functools.partial(one, p), 0)

    def drain(g, _):
        @pl.when(seq < last)
        def _():
            chain(0, g).wait_send()

        @pl.when(seq > 0)
        def _():
            chain(1, g).wait_send()

        for a in range(3):
            for off in offsets:
                cross(a, g, off).wait_send()
        return 0

    lax.fori_loop(0, groups, drain, 0)
    for slot in range(2):
        for r in range(strips):
            put(slot, r).wait()
    att_copy.wait()


def exchange(nseq, nhead, nsub, queries, key_rows, value_rows, out_adjoint):
    tok, heads, dim = queries.shape
    n = nhead * nsub
    tok_out = tok // n
    chunks = tok // CHUNK
    groups = heads // min(GROUP, heads)
    turned = pltpu.VMEM((heads, tok, dim), BF16)
    low = pltpu.VMEM((heads, dim, dim), BF16)
    any_spec = pl.BlockSpec(memory_space=pl.ANY)
    return pl.pallas_call(
        functools.partial(main_kernel, nseq, nhead, nsub),
        out_shape=(
            pltpu.VMEM((tok, heads, dim), BF16),
            pltpu.VMEM((2, tok_out, n * heads, dim), BF16),
            pltpu.VMEM((n, heads, tok_out, dim), BF16),
        ),
        in_specs=[any_spec] * 4,
        out_specs=(any_spec,) * 3,
        scratch_shapes=[
            pltpu.VMEM((4, tok, heads, dim), BF16),
            turned, turned, turned, turned,
            pltpu.VMEM((tok, dim), F32),
            pltpu.VMEM((heads, chunks, dim, dim), F32),
            pltpu.VMEM((heads, dim, dim), F32),
            pltpu.VMEM((heads, chunks, dim, dim), F32),
            pltpu.VMEM((heads, dim, dim), F32),
            low, low, low, low,
            pltpu.VMEM((3, heads, tok, dim), BF16),
            pltpu.VMEM((2, n, heads, tok_out, dim), BF16),
            pltpu.VMEM((2, tok_out, n * heads, dim), BF16),
            turned,
            pltpu.SemaphoreType.DMA((4, chunks)),
            pltpu.SemaphoreType.DMA((2, groups)),
            pltpu.SemaphoreType.DMA((2, groups)),
            pltpu.SemaphoreType.DMA((3, groups, n)),
            pltpu.SemaphoreType.DMA((3, groups, n)),
            pltpu.SemaphoreType.DMA((3, groups)),
            pltpu.SemaphoreType.DMA,
            pltpu.SemaphoreType.DMA((2, tok_out // min(16, tok_out))),
        ],
        compiler_params=pltpu.CompilerParams(
            collective_id=0, has_side_effects=True, vmem_limit_bytes=48 * 2**20
        ),
    )(key_rows, value_rows, out_adjoint, queries)


def finish_kernel(
    nseq, pieces, att, grads, late, att_out, qg_out, kg_out, vg_out, buf, stage, sem, in_sem, out_sem
):
    lower = lax.axis_index("seq") < (nseq + 1) // 2
    upper = jnp.logical_not(lower)
    n, heads, tok_out, dim = late.shape
    strip = tok_out // pieces

    def strip_rows(p):
        return pl.ds(p * strip, strip)

    def fetch(p):
        return pltpu.make_async_copy(
            late.at[:, :, strip_rows(p)], buf.at[:, :, strip_rows(p)], in_sem.at[p]
        )

    def copies(i, src, dst):
        step = dst.shape[0] // pieces
        rows = [pl.ds(p * step, step) for p in range(pieces)]
        return [
            pltpu.make_async_copy(src.at[r], dst.at[r], sem.at[i, p]) for p, r in enumerate(rows)
        ]

    def put(dst, p):
        return pltpu.make_async_copy(
            stage.at[strip_rows(p)], dst.at[strip_rows(p)], out_sem.at[p]
        )

    def turn(p):
        x = buf[:, :, strip_rows(p), :].reshape(n * heads, strip, dim)
        stage[strip_rows(p)] = jnp.swapaxes(x, 0, 1)

    def run(first, second, final):
        for p in range(pieces):
            fetch(p).start()
        rest = copies(0, grads.at[0], first) + copies(1, grads.at[1], second)
        rest += copies(2, att, att_out)
        for copy in rest:
            copy.start()
        for p in range(pieces):
            fetch(p).wait()
            turn(p)
            put(final, p).start()
        for copy in rest:
            copy.wait()
        for p in range(pieces):
            put(final, p).wait()

    @pl.when(lower)
    def _():
        run(qg_out, kg_out, vg_out)

    @pl.when(upper)
    def _():
        run(kg_out, vg_out, qg_out)


def finish(nseq, att, grads, late):
    tok_out = late.shape[2]
    pieces = max(1, min(4, tok_out // 16))
    any_spec = pl.BlockSpec(memory_space=pl.ANY)
    return pl.pallas_call(
        functools.partial(finish_kernel, nseq, pieces),
        out_shape=(jax.ShapeDtypeStruct(att.shape, BF16),)
        + (jax.ShapeDtypeStruct(grads.shape[1:], BF16),) * 3,
        in_specs=[any_spec] * 3,
        out_specs=(any_spec,) * 4,
        scratch_shapes=[
            pltpu.VMEM(late.shape, BF16),
            pltpu.VMEM(grads.shape[1:], BF16),
            pltpu.SemaphoreType.DMA((3, pieces)),
            pltpu.SemaphoreType.DMA((pieces,)),
            pltpu.SemaphoreType.DMA((pieces,)),
        ],
        compiler_params=pltpu.CompilerParams(vmem_limit_bytes=12 * 2**20),
    )(att, grads, late)


def solution(mesh):
    spec = P(("grp", "seq"), ("head", "sub"), None)
    grad = P(("grp", "seq", "head", "sub"), None, None)

    def per_device(queries, key_rows, value_rows, out_adjoint):
        return finish(
            mesh.shape["seq"],
            *exchange(
                mesh.shape["seq"], mesh.shape["head"], mesh.shape["sub"],
                queries, key_rows, value_rows, out_adjoint,
            ),
        )

    return jax.shard_map(
        per_device, mesh=mesh, in_specs=(spec,) * 4, out_specs=(spec, grad, grad, grad),
        check_vma=False,
    )
```
